512 devices in a mesh: section: 8 (over x, core), sp: 16 (over y, z_hi), cfg: 4 (over z_lo).
Axes of the slice: x: 4, y: 4, z: 16 (z_hi: 4, z_lo: 4; z = z_hi * 4 + z_lo), core: 2. Of those that a mesh axis runs over, the one named last changes fastest.
Arguments:
- queries: bfloat16 [16384, 2048], P(('section', 'sp', 'cfg')), may hold values from -112 to 112
- fresh_keys: bfloat16 [16384, 2048], P(('section', 'sp', 'cfg')), may hold values from -4 to 4
- fresh_values: bfloat16 [16384, 2048], P(('section', 'sp', 'cfg')), may hold values from -6 to 6
- stale_keys: bfloat16 [16, 16384, 128], P('sp', ('section', 'cfg')), may hold values from -6 to 6
- stale_values: bfloat16 [16, 16384, 128], P('sp', ('section', 'cfg')), may hold values from -6 to 6
- text_keys: bfloat16 [512, 2048], P('sp'), may hold values from -6 to 6
- text_values: bfloat16 [512, 2048], P('sp'), may hold values from -6 to 6
- order: int32 [8], replicated, may hold values from 0 to 1023
Outputs:
- attended: bfloat16 [16384, 2048], P(('section', 'sp', 'cfg'))
The draws below stay inside these ranges and needn't reach their ends.
All inputs are finite; a program needn't handle non-finite values.
Results may differ from the reference program's by a relative error of at most 0.006.
Values may be sent and summed in bfloat16 or wider, within the bound.
A program may use at most 64 MiB of HBM per device.

```python
import math
import jax
import jax.numpy as jnp
from jax import lax

H = 16
HD = 128
TXT = 512
IMG = 16384
PATCH = 2048
N_SECTION = 8


def shared_keys(key):
    return jnp.clip(jax.random.normal(key, (IMG, H * HD), jnp.float32), -4.0, 4.0)


def draw_fresh_keys(key, part):
    keys = shared_keys(key)
    return keys.astype(jnp.bfloat16)


def draw_queries(key, part):
    key = jax.random.fold_in(key, 11)
    base = 2.5 * jnp.clip(jax.random.normal(key, (IMG, H * HD), jnp.float32), -4.0, 4.0)
    return base.astype(jnp.bfloat16)


def touch_ends(entries, stream_key, least, largest):
    extent = entries.shape
    place = [jax.random.randint(jax.random.fold_in(stream_key, axis), (), 0, extent[axis]) for axis in range(len(extent))]
    entries = entries.at[tuple(place)].set(least)
    longest = extent.index(max(extent))
    place[longest] = (place[longest] + 1) % extent[longest]
    return entries.at[tuple(place)].set(largest)


def block_scale(rng, shape, split, low, largest):
    def one(position, shards_of):
        heights = jax.random.uniform(jax.random.fold_in(jax.random.fold_in(rng, 6), position), (shards_of,), jnp.float32, low / len(split), largest / len(split))
        return jnp.repeat(jnp.exp(heights), shape[position] // shards_of).reshape((-1,) + (1,) * (len(shape) - position - 1))

    gain = one(*split[0])
    for cut in split[1:]:
        gain = gain * one(*cut)
    return gain


def normal_values(rng, dims, deviation, most, cuts=(), kind=jnp.bfloat16):
    gain = block_scale(rng, dims, cuts, -0.22, 0.18) if cuts else 1.0
    array = jax.random.normal(rng, dims, jnp.float32) * deviation * gain
    return jnp.minimum(jnp.maximum(array, -most), most).astype(kind)


def setup_inputs(seed: int = 0) -> dict:
    key_list = jax.random.split(jax.random.key(seed), 9)
    return {
        "queries": draw_queries(jax.random.fold_in(key_list[8], 71), 0),
        "fresh_keys": draw_fresh_keys(jax.random.fold_in(key_list[8], 71), 0),
        "fresh_values": normal_values(key_list[2], (IMG, H * HD), 1.0, 6.0, ((0, 512),)),
        "stale_keys": normal_values(key_list[3], (H, IMG, HD), 1.0, 6.0, ((0, 16), (1, 32))),
        "stale_values": normal_values(key_list[4], (H, IMG, HD), 1.0, 6.0, ((0, 16), (1, 32))),
        "text_keys": normal_values(key_list[5], (TXT, H * HD), 1.0, 6.0, ((0, 16),)),
        "text_values": normal_values(key_list[6], (TXT, H * HD), 1.0, 6.0, ((0, 16),)),
        "order": touch_ends(jax.random.randint(key_list[7], (N_SECTION,), 0, 1024), jax.random.fold_in(key_list[7], 1), 0, 1023).astype(jnp.int32),
    }


def reference(queries, fresh_keys, fresh_values, stale_keys, stale_values, text_keys, text_values, order):
    score_scale = 1.0 / math.sqrt(HD)

    def by_head(matrix):
        return matrix.reshape(matrix.shape[0], H, HD).transpose(1, 0, 2)
    patch_of = jnp.arange(IMG, dtype=jnp.int32) // PATCH
    key_rank = order[patch_of]

    def one_head(bundle):
        head_q, head_fk, head_fv, head_sk, head_sv, head_tk, head_tv = bundle

        def one_patch(index):
            use_fresh = (key_rank <= order[index])[:, None]
            keys = jnp.concatenate([head_tk, jnp.where(use_fresh, head_fk, head_sk)], 0).astype(jnp.float32)
            values = jnp.concatenate([head_tv, jnp.where(use_fresh, head_fv, head_sv)], 0).astype(jnp.float32)
            rows = lax.dynamic_slice_in_dim(head_q, (index * PATCH).astype(jnp.int32), PATCH, 0).astype(jnp.float32)
            scores = jnp.dot(rows, keys.T, precision=lax.Precision.HIGHEST) * score_scale
            best = lax.optimization_barrier(jnp.max(scores, axis=1))
            weights = jnp.exp(scores - best[:, None])
            total = lax.optimization_barrier(jnp.sum(weights, axis=1))
            rounded = lax.optimization_barrier(weights.astype(jnp.bfloat16)).astype(jnp.float32)
            summed = jnp.dot(rounded, values, precision=lax.Precision.HIGHEST)
            return (summed / total[:, None]).astype(jnp.bfloat16)
        result = lax.map(one_patch, jnp.arange(N_SECTION, dtype=jnp.int32))
        return result.reshape(IMG, HD)
    bundle = (by_head(queries), by_head(fresh_keys), by_head(fresh_values), stale_keys, stale_values, by_head(text_keys), by_head(text_values))
    output = lax.map(one_head, bundle)
    return output.transpose(1, 0, 2).reshape(IMG, H * HD)
```

```python
import math

import jax
import jax.numpy as jnp
from jax import lax
from jax.experimental import pallas as pl
from jax.experimental.pallas import tpu as pltpu
from jax.sharding import PartitionSpec as P

MESH = pl.DeviceIdType.MESH
HD = 128
ROWS = 32
GROUP = 512
SEC = 8
TXT = 128
KEYS = SEC * GROUP + TXT
TILE = 256
SCALE2 = math.log2(math.e) / math.sqrt(HD)


def kernel(
    q_in, fk_in, fv_in, sk_in, sv_in, tk_in, tv_in, order,
    out,
    qg, fresh, stale, text, keys2, vals2, q2, sbuf, part, stats, got, got_stats, own, own_l, merged,
    sem_send, sem_q, sem_k, sem_v, sem_text, sem_stale, sem_xs, sem_xf, sem_cs, sem_cf, sem_y, sem_part, sem_stats,
    sem_out,
):
    sec = lax.axis_index("section")
    sp = lax.axis_index("sp")
    low = lax.axis_index("cfg")
    x, core = sec // 2, sec % 2
    y, high = sp // 4, sp % 4
    z = high * 4 + low

    def at_z(zz):
        return (sec, y * 4 + zz // 4, zz % 4)

    def at_y(yy):
        return (sec, yy * 4 + high, low)

    def at_sec(ss):
        return (ss, sp, low)

    def cols(head):
        return pl.ds(pl.multiple_of(head * HD, HD), HD)

    def rows(start, size):
        return pl.ds(pl.multiple_of(start, size), size)

    def head_of(zz):
        return (zz % 4) * 4 + zz // 4

    def remote(src, dst, recv, target):
        copy = pltpu.make_async_remote_copy(
            src_ref=src, dst_ref=dst, send_sem=sem_send.at[0], recv_sem=recv, device_id=target, device_id_type=MESH
        )
        copy.start()

    def arrived(ref, sem):
        pltpu.make_async_copy(ref, ref, sem).wait()

    sibling = sec + 1 - 2 * core
    across = [lax.rem(x + d, 4) * 2 + core for d in range(1, 4)]

    barrier = pltpu.get_barrier_semaphore()

    def greet(target):
        pl.semaphore_signal(barrier, inc=1, device_id=target, device_id_type=MESH)

    for d in (8, 7, 9, 6, 10, 5, 11, 4, 12, 3, 13, 2, 14, 1, 15):
        greet(at_z(lax.rem(z + d, 16)))
    for d in range(1, 4):
        greet(at_y(lax.rem(y + d, 4)))
    for s in across:
        greet(at_sec(s))
    greet(at_sec(sibling))

    @pl.when(low != y)
    def _():
        for c in range(4):
            greet((sec, low * 4 + high, c))

    pl.semaphore_wait(barrier, 25)

    for kv, src in enumerate((sk_in, sv_in)):
        for k in range(1, 4):
            r = lax.rem(y + k, 4)
            remote(src.at[0, rows(r * 128, 128)], stale.at[sec, kv, rows(low * 128, 128)], sem_stale.at[0], (sec, r * 4 + high, y))

        @pl.when(low != y)
        def _():
            remote(src.at[0, rows(y * 128, 128)], stale.at[sec, kv, rows(low * 128, 128)], sem_stale.at[0], (sec, sp, y))

        @pl.when(low == y)
        def _():
            pltpu.make_async_copy(src.at[0, rows(y * 128, 128)], stale.at[sec, kv, rows(low * 128, 128)], sem_stale.at[0]).start()

    mine = cols(head_of(z))
    place = rows(z * ROWS, ROWS)
    for src, dst, sem in ((fk_in, fresh.at[sec, 0], sem_k), (fv_in, fresh.at[sec, 1], sem_v), (q_in, qg.at[y], sem_q)):
        pltpu.make_async_copy(src.at[:, mine], dst.at[place], sem.at[0]).start()
        for d in (8, 7, 9, 6, 10, 5, 11, 4, 12, 3, 13, 2, 14, 1, 15):
            zz = lax.rem(z + d, 16)
            remote(src.at[:, cols(head_of(zz))], dst.at[place], sem.at[0], at_z(zz))
    text_place = rows(high * ROWS, ROWS)
    for kv, src in enumerate((tk_in, tv_in)):
        pltpu.make_async_copy(src.at[:, mine], text.at[kv, text_place], sem_text.at[0]).start()
        for d in (2, 1, 3):
            a = lax.rem(high + d, 4)
            remote(src.at[:, cols(low * 4 + a)], text.at[kv, text_place], sem_text.at[0], (sec, y * 4 + a, low))

    def spread(block, sem_x, sem_c):
        for i, s in enumerate(across):
            remote(block.at[sec], block.at[sec], sem_x.at[i], at_sec(s))
        remote(block.at[sec], block.at[sec], sem_c.at[3], at_sec(sibling))

    def forward(block, sem_x, sem_c):
        for i in (0, 2, 1):
            s = lax.rem(x + 3 - i, 4) * 2 + core
            arrived(block.at[s], sem_x.at[i])
            remote(block.at[s], block.at[s], sem_c.at[i], at_sec(sibling))

    arrived(stale.at[sec], sem_stale.at[0])
    spread(stale, sem_xs, sem_cs)
    arrived(fresh.at[sec, 0], sem_k.at[0])
    arrived(fresh.at[sec, 1], sem_v.at[0])
    spread(fresh, sem_xf, sem_cf)
    arrived(qg.at[y], sem_q.at[0])
    for k in range(1, 4):
        remote(qg.at[y], qg.at[y], sem_y.at[k - 1], at_y(lax.rem(y + k, 4)))
    forward(stale, sem_xs, sem_cs)
    arrived(text, sem_text.at[0])
    vals2[:, HD:] = jnp.ones((KEYS, HD), jnp.bfloat16)
    keys2[SEC * GROUP :, :HD] = text[0]
    keys2[SEC * GROUP :, HD:] = text[0]
    vals2[SEC * GROUP :, :HD] = text[1]
    forward(fresh, sem_xf, sem_cf)
    for i in range(4):
        s = lax.rem(x + 3 - i + 4, 4) * 2 + 1 - core
        arrived(stale.at[s], sem_cs.at[i])
        arrived(fresh.at[s], sem_cf.at[i])

    my_order = order[sec]
    for j in range(SEC):
        use_fresh = order[j] <= my_order
        block = pl.ds(j * GROUP, GROUP)
        chosen = jnp.where(use_fresh, fresh[j, 0], stale[j, 0])
        keys2[block, :HD] = chosen
        keys2[block, HD:] = chosen
        vals2[block, :HD] = jnp.where(use_fresh, fresh[j, 1], stale[j, 1])

    def scaled(yy):
        wide = qg[yy].astype(jnp.float32) * SCALE2
        first = wide.astype(jnp.bfloat16)
        q2[yy, :, :HD] = first
        q2[yy, :, HD:] = (wide - first.astype(jnp.float32)).astype(jnp.bfloat16)

    scaled(y)
    for k in range(1, 4):
        yy = lax.rem(y + 4 - k, 4)
        arrived(qg.at[yy], sem_y.at[k - 1])
        scaled(yy)

    def tile_of(t):
        return lax.rem(y + 1 + t, 4), t // 4

    def scores(t):
        yy, half = tile_of(t)
        return lax.dot_general(
            q2[yy, rows(half * TILE, TILE), :], keys2[...], (((1,), (1,)), ((), ())), preferred_element_type=jnp.float32
        )

    def finish(t, s):
        yy, half = tile_of(t)
        best = jnp.max(s, axis=1, keepdims=True)
        weights = jnp.exp2(s - best).astype(jnp.bfloat16)
        both = jnp.dot(weights, vals2[...], preferred_element_type=jnp.float32)
        total = both[:, HD:]
        value = both[:, :HD] / total
        level = best + jnp.log2(total)
        return yy, half, value, level

    def give(t, s):
        yy, half, value, level = finish(t, s)
        part[yy, rows(half * TILE, TILE), :] = value.astype(jnp.bfloat16)
        stats[yy, half] = jnp.transpose(level)[:8]
        remote(part.at[yy, rows(half * TILE, TILE)], got.at[y, rows(half * TILE, TILE)], sem_part.at[half, y], at_y(yy))
        remote(stats.at[yy, half], got_stats.at[y, half], sem_stats.at[half, y], at_y(yy))

    def keep(t, s):
        yy, half, value, level = finish(t, s)
        own[half] = value
        own_l[half] = level

    def merge(half):
        here = rows(half * TILE, TILE)
        levels, values = [own_l[half]], [own[half]]
        for k in range(1, 4):
            yy = lax.rem(y + k, 4)
            arrived(got.at[yy, here], sem_part.at[half, yy])
            arrived(got_stats.at[yy, half], sem_stats.at[half, yy])
            level = got_stats[yy, half]
            levels.append(jnp.transpose(jnp.broadcast_to(level[:1], (HD, TILE))))
            values.append(got[yy, here, :].astype(jnp.float32))
        top = jnp.maximum(jnp.maximum(levels[0], levels[1]), jnp.maximum(levels[2], levels[3]))
        shares = [jnp.exp2(level - top) for level in levels]
        total = shares[0] + shares[1] + shares[2] + shares[3]
        summed = shares[0] * values[0] + shares[1] * values[1] + shares[2] * values[2] + shares[3] * values[3]
        merged[here, :] = (summed / total).astype(jnp.bfloat16)
        for d in range(8):
            zz = half * 8 + d
            src = merged.at[rows(zz * ROWS, ROWS)]

            @pl.when(zz == z)
            def _():
                pltpu.make_async_copy(src, out.at[:, mine], sem_out.at[0]).start()

            @pl.when(zz != z)
            def _():
                remote(src, out.at[:, mine], sem_out.at[0], at_z(zz))

    sbuf[0] = scores(0)

    def pair(u, _):
        @pl.when(u == 3)
        def _():
            merge(0)

        t = u * 2
        sbuf[1] = scores(t + 1)
        give(t, sbuf[0])
        sbuf[0] = scores(jnp.minimum(t + 2, 7))

        @pl.when(u % 2 == 0)
        def _():
            give(t + 1, sbuf[1])

        @pl.when(u % 2 == 1)
        def _():
            keep(t + 1, sbuf[1])

        return 0

    lax.fori_loop(0, 4, pair, 0)
    merge(1)

    arrived(out, sem_out.at[0])

    def sent(ref):
        pltpu.make_async_copy(ref, ref, sem_send.at[0]).wait()

    sent(stale.at[0, :, pl.ds(0, 384)])

    @pl.when(low != y)
    def _():
        sent(stale.at[0, :, pl.ds(0, 128)])

    for _ in range(4):
        sent(qg.at[0, pl.ds(0, 480)])
    sent(text.at[:, pl.ds(0, 96)])
    for _ in range(14):
        sent(stale.at[0])
    for _ in range(3):
        sent(qg.at[0])
    for _ in range(3):
        sent(qg.at[0])
        sent(stats.at[0])


def local(queries, fresh_keys, fresh_values, stale_keys, stale_values, text_keys, text_values, order):
    anywhere = pl.BlockSpec(memory_space=pl.ANY)
    dma = pltpu.SemaphoreType.DMA
    bf16, f32 = jnp.bfloat16, jnp.float32
    return pl.pallas_call(
        kernel,
        out_shape=jax.ShapeDtypeStruct((ROWS, 16 * HD), bf16),
        in_specs=[anywhere] * 7 + [pl.BlockSpec(memory_space=pltpu.SMEM)],
        out_specs=anywhere,
        scratch_shapes=[
            pltpu.VMEM((4, GROUP, HD), bf16),
            pltpu.VMEM((SEC, 2, GROUP, HD), bf16),
            pltpu.VMEM((SEC, 2, GROUP, HD), bf16),
            pltpu.VMEM((2, TXT, HD), bf16),
            pltpu.VMEM((KEYS, 2 * HD), bf16),
            pltpu.VMEM((KEYS, 2 * HD), bf16),
            pltpu.VMEM((4, GROUP, 2 * HD), bf16),
            pltpu.VMEM((2, TILE, KEYS), f32),
            pltpu.VMEM((4, GROUP, HD), bf16),
            pltpu.VMEM((4, 2, 8, TILE), f32),
            pltpu.VMEM((4, GROUP, HD), bf16),
            pltpu.VMEM((4, 2, 8, TILE), f32),
            pltpu.VMEM((2, TILE, HD), f32),
            pltpu.VMEM((2, TILE, HD), f32),
            pltpu.VMEM((GROUP, HD), bf16),
            dma((1,)),
            dma((1,)),
            dma((1,)),
            dma((1,)),
            dma((1,)),
            dma((1,)),
            dma((3,)),
            dma((3,)),
            dma((4,)),
            dma((4,)),
            dma((3,)),
            dma((2, 4)),
            dma((2, 4)),
            dma((1,)),
        ],
        compiler_params=pltpu.CompilerParams(collective_id=0, has_side_effects=True, vmem_limit_bytes=56 << 20),
    )(queries, fresh_keys, fresh_values, stale_keys, stale_values, text_keys, text_values, order)


def solution(mesh):
    return jax.shard_map(
        local,
        mesh=mesh,
        in_specs=(
            P(("section", "sp", "cfg"), None),
            P(("section", "sp", "cfg"), None),
            P(("section", "sp", "cfg"), None),
            P("sp", ("section", "cfg"), None),
            P("sp", ("section", "cfg"), None),
            P("sp", None),
            P("sp", None),
            P(),
        ),
        out_specs=P(("section", "sp", "cfg"), None),
        check_vma=False,
    )
```

```python
import math

import jax
import jax.numpy as jnp
from jax import lax
from jax.experimental import pallas as pl
from jax.experimental.pallas import tpu as pltpu
from jax.sharding import PartitionSpec as P

MESH = pl.DeviceIdType.MESH
HD = 128
ROWS = 32
GROUP = 512
SEC = 8
TXT = 128
KEYS = SEC * GROUP + TXT
FAR_FIRST = (8, 7, 9, 6, 10, 5, 11, 4, 12, 3, 13, 2, 14, 1, 15)
TILE = 256
SCALE2 = math.log2(math.e) / math.sqrt(HD)


def kernel(
    q_in, fk_in, fv_in, sk_in, sv_in, tk_in, tv_in, order,
    out,
    qg, fresh, stale, hop, text, keys2, vals2, q2, sbuf, part, stats, got, got_stats, own, own_l, merged,
    sem_send, sem_q, sem_k, sem_v, sem_text, sem_stale, sem_u, sem_hop, sem_y, sem_part, sem_stats,
    sem_out,
):
    sec = lax.axis_index("section")
    sp = lax.axis_index("sp")
    low = lax.axis_index("cfg")
    x, core = sec // 2, sec % 2
    y, high = sp // 4, sp % 4
    z = high * 4 + low

    def at_z(zz):
        return (sec, y * 4 + zz // 4, zz % 4)

    def at_y(yy):
        return (sec, yy * 4 + high, low)

    def at_sec(ss):
        return (ss, sp, low)

    def cols(head):
        return pl.ds(pl.multiple_of(head * HD, HD), HD)

    def rows(start, size):
        return pl.ds(pl.multiple_of(start, size), size)

    def head_of(zz):
        return (zz % 4) * 4 + zz // 4

    def remote(src, dst, recv, target):
        copy = pltpu.make_async_remote_copy(
            src_ref=src, dst_ref=dst, send_sem=sem_send.at[0], recv_sem=recv, device_id=target, device_id_type=MESH
        )
        copy.start()

    def arrived(ref, sem):
        pltpu.make_async_copy(ref, ref, sem).wait()

    sibling = sec + 1 - 2 * core
    right, opposite, left = [lax.rem(x + d, 4) * 2 + core for d in range(1, 4)]

    barrier = pltpu.get_barrier_semaphore()

    def greet(target):
        pl.semaphore_signal(barrier, inc=1, device_id=target, device_id_type=MESH)

    for d in FAR_FIRST:
        greet(at_z(lax.rem(z + d, 16)))
    for d in range(1, 4):
        greet(at_y(lax.rem(y + d, 4)))
    greet(at_sec(right))
    greet(at_sec(left))
    greet(at_sec(sibling))
    pl.semaphore_wait(barrier, 21)

    for k in (2, 1, 3):
        r = lax.rem(y + k, 4)
        for kv, src in enumerate((sk_in, sv_in)):
            remote(src.at[0, rows(r * 128, 128)], hop.at[y, kv], sem_hop.at[k - 1], at_y(r))

    mine = cols(head_of(z))
    place = rows(z * ROWS, ROWS)

    def to_heads(src, dst, sem, by_distance):
        pltpu.make_async_copy(src.at[:, mine], dst.at[rows(4 * ROWS, ROWS) if by_distance else place], sem.at[0]).start()
        for d in FAR_FIRST:
            zz = lax.rem(z + d, 16)
            there = rows((4 - d) % 16 * ROWS, ROWS) if by_distance else place
            remote(src.at[:, cols(head_of(zz))], dst.at[there], sem.at[0], at_z(zz))

    stale_rows = rows(low * 128, 128)

    def swap():
        @pl.when(low != y)
        def _():
            for kv, src in enumerate((sk_in, sv_in)):
                remote(src.at[0, rows(y * 128, 128)], stale.at[sec, kv, stale_rows], sem_stale.at[0], (sec, sp, y))

        @pl.when(low == y)
        def _():
            for kv, src in enumerate((sk_in, sv_in)):
                pltpu.make_async_copy(src.at[0, rows(y * 128, 128)], stale.at[sec, kv, stale_rows], sem_stale.at[0]).start()

        for k in (1, 3, 2):
            yy = lax.rem(y + 4 - k, 4)
            arrived(hop.at[yy], sem_hop.at[k - 1])

            @pl.when(low != yy)
            def _():
                remote(hop.at[yy], stale.at[sec, :, stale_rows], sem_stale.at[0], (sec, sp, yy))

            @pl.when(low == yy)
            def _():
                pltpu.make_async_copy(hop.at[yy], stale.at[sec, :, stale_rows], sem_stale.at[0]).start()

    text_place = rows(high * ROWS, ROWS)

    def send_text():
        for kv, src in enumerate((tk_in, tv_in)):
            pltpu.make_async_copy(src.at[:, mine], text.at[kv, text_place], sem_text.at[0]).start()
            for d in (2, 1, 3):
                a = lax.rem(high + d, 4)
                remote(src.at[:, cols(low * 4 + a)], text.at[kv, text_place], sem_text.at[0], (sec, y * 4 + a, low))

    upper, lower = pl.ds(0, 256), pl.ds(256, 256)
    from_left, from_right = left, right

    def spread(part_of, sems):
        block = part_of(sec)
        remote(block, block, sems.at[0], at_sec(right))
        remote(block, block, sems.at[1], at_sec(left))
        remote(block, block, sems.at[4], at_sec(sibling))

    def forward(part_of, half_of, sems):
        block = part_of(from_left)
        arrived(block, sems.at[0])
        half = half_of(from_left, upper)
        remote(half, half, sems.at[2], at_sec(right))
        remote(block, block, sems.at[5], at_sec(sibling))
        block = part_of(from_right)
        arrived(block, sems.at[1])
        half = half_of(from_right, lower)
        remote(half, half, sems.at[3], at_sec(left))
        remote(block, block, sems.at[6], at_sec(sibling))

    def forward_far(half_of, sems):
        half = half_of(opposite, upper)
        arrived(half, sems.at[2])
        remote(half, half, sems.at[7], at_sec(sibling))
        half = half_of(opposite, lower)
        arrived(half, sems.at[3])
        remote(half, half, sems.at[8], at_sec(sibling))

    def all_here(part_of, half_of, sems):
        arrived(part_of(sibling), sems.at[4])
        arrived(part_of(from_left + other), sems.at[5])
        arrived(part_of(from_right + other), sems.at[6])
        arrived(half_of(opposite + other, upper), sems.at[7])
        arrived(half_of(opposite + other, lower), sems.at[8])

    other = 1 - 2 * core
    keys_unit = (lambda s: fresh.at[s, 0], lambda s, h: fresh.at[s, 0, h], sem_u.at[0])
    vals_unit = (lambda s: fresh.at[s, 1], lambda s, h: fresh.at[s, 1, h], sem_u.at[1])
    stale_unit = (lambda s: stale.at[s], lambda s, h: stale.at[s, :, h], sem_u.at[2])

    def do_spread(unit):
        spread(unit[0], unit[2])

    def do_forward(unit):
        forward(*unit)

    def do_far(unit):
        forward_far(unit[1], unit[2])

    to_heads(fk_in, fresh.at[sec, 0], sem_k, False)
    to_heads(fv_in, fresh.at[sec, 1], sem_v, False)
    swap()
    to_heads(q_in, qg.at[y], sem_q, True)
    send_text()
    arrived(fresh.at[sec, 0], sem_k.at[0])
    do_spread(keys_unit)
    arrived(stale.at[sec], sem_stale.at[0])
    do_spread(stale_unit)
    arrived(fresh.at[sec, 1], sem_v.at[0])
    do_spread(vals_unit)
    do_forward(keys_unit)
    arrived(qg.at[y], sem_q.at[0])
    for k in (2, 1, 3):
        remote(qg.at[y], qg.at[y], sem_y.at[k - 1], at_y(lax.rem(y + k, 4)))
    do_forward(stale_unit)
    do_forward(vals_unit)
    do_far(keys_unit)
    arrived(text, sem_text.at[0])
    vals2[:, HD:] = jnp.ones((KEYS, HD), jnp.bfloat16)
    keys2[SEC * GROUP :, :HD] = text[0]
    keys2[SEC * GROUP :, HD:] = text[0]
    vals2[SEC * GROUP :, :HD] = text[1]
    do_far(stale_unit)
    do_far(vals_unit)
    for unit in (keys_unit, stale_unit, vals_unit):
        all_here(*unit)

    my_order = order[sec]
    for j in range(SEC):
        use_fresh = order[j] <= my_order
        block = pl.ds(j * GROUP, GROUP)
        chosen = jnp.where(use_fresh, fresh[j, 0], stale[j, 0])
        keys2[block, :HD] = chosen
        keys2[block, HD:] = chosen
        vals2[block, :HD] = jnp.where(use_fresh, fresh[j, 1], stale[j, 1])

    def scaled(yy):
        wide = qg[yy].astype(jnp.float32) * SCALE2
        first = wide.astype(jnp.bfloat16)
        q2[yy, :, :HD] = first
        q2[yy, :, HD:] = (wide - first.astype(jnp.float32)).astype(jnp.bfloat16)

    scaled(y)
    for k in range(1, 4):
        yy = lax.rem(y + 4 - k, 4)
        arrived(qg.at[yy], sem_y.at[k - 1])
        scaled(yy)

    def tile_of(t):
        return lax.rem(y + 1 + t, 4), t // 4

    def scores(t):
        yy, half = tile_of(t)
        return lax.dot_general(
            q2[yy, rows((1 - half) * TILE, TILE), :], keys2[...], (((1,), (1,)), ((), ())), preferred_element_type=jnp.float32
        )

    def finish(t, s):
        yy, half = tile_of(t)
        best = jnp.max(s, axis=1, keepdims=True)
        weights = jnp.exp2(s - best).astype(jnp.bfloat16)
        both = jnp.dot(weights, vals2[...], preferred_element_type=jnp.float32)
        total = both[:, HD:]
        value = both[:, :HD] / total
        level = best + jnp.log2(total)
        return yy, half, value, level

    def give(t, s):
        yy, half, value, level = finish(t, s)
        part[yy, rows(half * TILE, TILE), :] = value.astype(jnp.bfloat16)
        stats[yy, half] = jnp.transpose(level)[:8]
        remote(part.at[yy, rows(half * TILE, TILE)], got.at[y, rows(half * TILE, TILE)], sem_part.at[half, y], at_y(yy))
        remote(stats.at[yy, half], got_stats.at[y, half], sem_stats.at[half, y], at_y(yy))

    def keep(t, s):
        yy, half, value, level = finish(t, s)
        own[half] = value
        own_l[half] = level

    def merge(half):
        here = rows(half * TILE, TILE)
        levels, values = [own_l[half]], [own[half]]
        for k in range(1, 4):
            yy = lax.rem(y + k, 4)
            arrived(got.at[yy, here], sem_part.at[half, yy])
            arrived(got_stats.at[yy, half], sem_stats.at[half, yy])
            level = got_stats[yy, half]
            levels.append(jnp.transpose(jnp.broadcast_to(level[:1], (HD, TILE))))
            values.append(got[yy, here, :].astype(jnp.float32))
        top = jnp.maximum(jnp.maximum(levels[0], levels[1]), jnp.maximum(levels[2], levels[3]))
        shares = [jnp.exp2(level - top) for level in levels]
        total = shares[0] + shares[1] + shares[2] + shares[3]
        summed = shares[0] * values[0] + shares[1] * values[1] + shares[2] * values[2] + shares[3] * values[3]
        merged[here, :] = (summed / total).astype(jnp.bfloat16)
        for d in (0, 7, 1, 6, 2, 5, 3, 4):
            off = (1 - half) * 8 + d - 4
            src = merged.at[pl.ds(half * TILE + d * ROWS, ROWS)]
            if off == 0:
                pltpu.make_async_copy(src, out.at[:, mine], sem_out.at[0]).start()
            else:
                remote(src, out.at[:, mine], sem_out.at[0], at_z(lax.rem(z + off + 16, 16)))

    sbuf[0] = scores(0)

    def pair(u, _):
        @pl.when(u == 3)
        def _():
            merge(0)

        t = u * 2
        sbuf[1] = scores(t + 1)
        give(t, sbuf[0])
        sbuf[0] = scores(jnp.minimum(t + 2, 7))

        @pl.when(u % 2 == 0)
        def _():
            give(t + 1, sbuf[1])

        @pl.when(u % 2 == 1)
        def _():
            keep(t + 1, sbuf[1])

        return 0

    lax.fori_loop(0, 4, pair, 0)
    merge(1)

    arrived(out, sem_out.at[0])

    def sent(ref):
        pltpu.make_async_copy(ref, ref, sem_send.at[0]).wait()

    for _ in range(2):
        sent(stale.at[0, :, pl.ds(0, 384)])
    for _ in range(4):
        sent(qg.at[0, pl.ds(0, 480)])
    sent(text.at[:, pl.ds(0, 96)])
    for _ in range(14):
        sent(stale.at[0])
    for _ in range(3):
        sent(qg.at[0])
    for _ in range(3):
        sent(qg.at[0])
        sent(stats.at[0])


def local(queries, fresh_keys, fresh_values, stale_keys, stale_values, text_keys, text_values, order):
    anywhere = pl.BlockSpec(memory_space=pl.ANY)
    dma = pltpu.SemaphoreType.DMA
    bf16, f32 = jnp.bfloat16, jnp.float32
    return pl.pallas_call(
        kernel,
        out_shape=jax.ShapeDtypeStruct((ROWS, 16 * HD), bf16),
        in_specs=[anywhere] * 7 + [pl.BlockSpec(memory_space=pltpu.SMEM)],
        out_specs=anywhere,
        scratch_shapes=[
            pltpu.VMEM((4, GROUP, HD), bf16),
            pltpu.VMEM((SEC, 2, GROUP, HD), bf16),
            pltpu.VMEM((SEC, 2, GROUP, HD), bf16),
            pltpu.VMEM((4, 2, 128, HD), bf16),
            pltpu.VMEM((2, TXT, HD), bf16),
            pltpu.VMEM((KEYS, 2 * HD), bf16),
            pltpu.VMEM((KEYS, 2 * HD), bf16),
            pltpu.VMEM((4, GROUP, 2 * HD), bf16),
            pltpu.VMEM((2, TILE, KEYS), f32),
            pltpu.VMEM((4, GROUP, HD), bf16),
            pltpu.VMEM((4, 2, 8, TILE), f32),
            pltpu.VMEM((4, GROUP, HD), bf16),
            pltpu.VMEM((4, 2, 8, TILE), f32),
            pltpu.VMEM((2, TILE, HD), f32),
            pltpu.VMEM((2, TILE, HD), f32),
            pltpu.VMEM((GROUP, HD), bf16),
            dma((1,)),
            dma((1,)),
            dma((1,)),
            dma((1,)),
            dma((1,)),
            dma((1,)),
            dma((3, 9)),
            dma((3,)),
            dma((3,)),
            dma((2, 4)),
            dma((2, 4)),
            dma((1,)),
        ],
        compiler_params=pltpu.CompilerParams(collective_id=0, has_side_effects=True, vmem_limit_bytes=56 << 20),
    )(queries, fresh_keys, fresh_values, stale_keys, stale_values, text_keys, text_values, order)


def solution(mesh):
    return jax.shard_map(
        local,
        mesh=mesh,
        in_specs=(
            P(("section", "sp", "cfg"), None),
            P(("section", "sp", "cfg"), None),
            P(("section", "sp", "cfg"), None),
            P("sp", ("section", "cfg"), None),
            P("sp", ("section", "cfg"), None),
            P("sp", None),
            P("sp", None),
            P(),
        ),
        out_specs=P(("section", "sp", "cfg"), None),
        check_vma=False,
    )
```

```python
import math

import jax
import jax.numpy as jnp
from jax import lax
from jax.experimental import pallas as pl
from jax.experimental.pallas import tpu as pltpu
from jax.sharding import PartitionSpec as P

MESH = pl.DeviceIdType.MESH
HD = 128
ROWS = 32
GROUP = 512
SEC = 8
TXT = 128
KEYS = SEC * GROUP + TXT
HALF = SEC * GROUP // 2
FIRST, SECOND = pl.ds(0, HALF), pl.ds(HALF, HALF + TXT)
FAR_FIRST = (8, 7, 9, 6, 10, 5, 11, 4, 12, 3, 13, 2, 14, 1, 15)
TILE = 256
SCALE2 = math.log2(math.e) / math.sqrt(HD)


def kernel(
    q_in, fk_in, fv_in, sk_in, sv_in, tk_in, tv_in, order,
    out,
    qg, fresh, stale, hop, text, keys2, vals2, q2, sbuf, so_far, best_so_far, partial, stats, got, got_stats, own, own_l, merged,
    sem_send, sem_q, sem_f, sem_text, sem_stale, sem_u, sem_hop, sem_y, sem_part, sem_stats,
    sem_out,
):
    sec = lax.axis_index("section")
    sp = lax.axis_index("sp")
    low = lax.axis_index("cfg")
    x, core = sec // 2, sec % 2
    y, high = sp // 4, sp % 4
    z = high * 4 + low

    def at_z(zz):
        return (sec, y * 4 + zz // 4, zz % 4)

    def at_y(yy):
        return (sec, yy * 4 + high, low)

    def at_sec(ss):
        return (ss, sp, low)

    def cols(head):
        return pl.ds(pl.multiple_of(head * HD, HD), HD)

    def rows(start, size):
        return pl.ds(start if isinstance(start, int) else pl.multiple_of(start, size), size)

    def head_of(zz):
        return (zz % 4) * 4 + zz // 4

    def remote(src, dst, recv, target):
        copy = pltpu.make_async_remote_copy(
            src_ref=src, dst_ref=dst, send_sem=sem_send.at[0], recv_sem=recv, device_id=target, device_id_type=MESH
        )
        copy.start()

    def arrived(ref, sem):
        pltpu.make_async_copy(ref, ref, sem).wait()

    sibling = sec + 1 - 2 * core
    right, opposite, left = [lax.rem(x + d, 4) * 2 + core for d in range(1, 4)]

    barrier = pltpu.get_barrier_semaphore()

    def greet(target):
        pl.semaphore_signal(barrier, inc=1, device_id=target, device_id_type=MESH)

    for d in FAR_FIRST:
        greet(at_z(lax.rem(z + d, 16)))
    for d in range(1, 4):
        greet(at_y(lax.rem(y + d, 4)))
    greet(at_sec(right))
    greet(at_sec(left))
    greet(at_sec(sibling))
    pl.semaphore_wait(barrier, 21)


    pending = {}
    count = [0]

    def units_of(ref):
        n = 1
        for d in ref.shape:
            n *= d
        return n // (ROWS * HD)

    def put(src, dst, recv, target):
        remote(src, dst, recv, target)
        count[0] += units_of(src)

    def expect(name, ref, sem):
        pending[name] = (ref, sem)

    def await_(name):
        arrived(*pending.pop(name))

    for k in (2, 1, 3):
        r = lax.rem(y + k, 4)
        for kv, src in enumerate((sk_in, sv_in)):
            put(src.at[0, rows(r * 128, 128)], hop.at[y, kv], sem_hop.at[k - 1], at_y(r))
        expect(f"hop{k}", hop.at[lax.rem(y + 4 - k, 4)], sem_hop.at[k - 1])

    mine = cols(head_of(z))

    def to_heads(src, dst, sem, distances, place):
        for d in distances:
            if d == 0:
                pltpu.make_async_copy(src.at[:, mine], dst.at[place(d)], sem).start()
            else:
                zz = lax.rem(z + d, 16)
                put(src.at[:, cols(head_of(zz))], dst.at[place(d)], sem, at_z(zz))

    to_heads(q_in, qg.at[y], sem_q.at[0], (0,) + FAR_FIRST, lambda d: rows(z * ROWS, ROWS))
    expect("q", qg.at[y], sem_q.at[0])

    stale_rows = rows(low * 128, 128)

    @pl.when(low != y)
    def _():
        for kv, src in enumerate((sk_in, sv_in)):
            remote(src.at[0, rows(y * 128, 128)], stale.at[sec, kv, stale_rows], sem_stale.at[0], (sec, sp, y))

    @pl.when(low == y)
    def _():
        for kv, src in enumerate((sk_in, sv_in)):
            pltpu.make_async_copy(src.at[0, rows(y * 128, 128)], stale.at[sec, kv, stale_rows], sem_stale.at[0]).start()

    for k in (1, 3, 2):
        yy = lax.rem(y + 4 - k, 4)
        await_(f"hop{k}")

        @pl.when(low != yy)
        def _():
            remote(hop.at[yy], stale.at[sec, :, stale_rows], sem_stale.at[0], (sec, sp, yy))

        @pl.when(low == yy)
        def _():
            pltpu.make_async_copy(hop.at[yy], stale.at[sec, :, stale_rows], sem_stale.at[0]).start()

    count[0] += 3 * 8
    expect("s", stale.at[sec], sem_stale.at[0])

    for name, i, distances in (("e", 0, (8, 6, 10, 4, 12, 2, 14, 0)), ("o", 1, (7, 9, 5, 11, 3, 13, 1, 15))):
        for kv, src in enumerate((fk_in, fv_in)):
            to_heads(src, fresh.at[sec, kv], sem_f.at[i], distances, lambda d: pl.ds((d % 2 * 8 + d // 2) * ROWS, ROWS))
        expect(name, fresh.at[sec, :, pl.ds(i * 256, 256)], sem_f.at[i])

    def text_rows(xx):
        return text.at[:, rows(xx * ROWS, ROWS)]

    text_mine = text_rows(x)

    @pl.when(high == x)
    def _():
        for kv, src in enumerate((tk_in, tv_in)):
            pltpu.make_async_copy(src.at[:, mine], text.at[kv, rows(x * ROWS, ROWS)], sem_text.at[0]).start()
            for d in (2, 1, 3):
                a = lax.rem(high + d, 4)
                there = text.at[kv, rows(x * ROWS, ROWS)]
                remote(src.at[:, cols(low * 4 + a)], there, sem_text.at[0], (sec, y * 4 + a, low))

    expect("t", text_mine, sem_text.at[0])

    text_to = [None] + [at_sec(lax.rem(x + d, 4) * 2 + core) for d in range(1, 4)]
    text_from = [None] + [text_rows(lax.rem(x + 4 - d, 4)) for d in range(1, 4)]

    def spread_text():
        await_("t")
        for d in (2, 1, 3):
            put(text_mine, text_mine, sem_text.at[d], text_to[d])
            expect(f"t{d}", text_from[d], sem_text.at[d])

    other = 1 - 2 * core
    left2, right2, opposite2 = left + other, right + other, opposite + other
    units = {"s": (stale, 0, 512, 0), "e": (fresh, 0, 256, 1), "o": (fresh, 256, 256, 2)}

    def part(u, s, half=None):
        ref, start, size, _ = units[u]
        if half is not None:
            start, size = start + half * size // 2, size // 2
        return ref.at[s, :, pl.ds(start, size)]

    def pass_on(u, i, ref, to, expected):
        sem = sem_u.at[units[u][3], i]
        put(ref, ref, sem, at_sec(to))
        expect(u + str(i), expected, sem)

    def spread(u):
        await_(u)
        block = part(u, sec)
        pass_on(u, 0, block, right, part(u, left))
        pass_on(u, 1, block, left, part(u, right))
        pass_on(u, 4, block, sibling, part(u, sibling))

    def forward(u):
        await_(u + "0")
        pass_on(u, 2, part(u, left, 0), right, part(u, opposite, 0))
        pass_on(u, 5, part(u, left), sibling, part(u, left2))
        await_(u + "1")
        pass_on(u, 3, part(u, right, 1), left, part(u, opposite, 1))
        pass_on(u, 6, part(u, right), sibling, part(u, right2))

    def forward_far(u):
        for i in range(2):
            await_(u + str(2 + i))
            pass_on(u, 7 + i, part(u, opposite, i), sibling, part(u, opposite2, i))

    def all_here(u):
        for i in range(4, 9):
            await_(u + str(i))

    vals2[:, HD:] = jnp.ones((KEYS, HD), jnp.bfloat16)
    await_("q")
    for k in (2, 1, 3):
        put(qg.at[y], qg.at[y], sem_y.at[k - 1], at_y(lax.rem(y + k, 4)))
        expect(f"q{k}", qg.at[lax.rem(y + 4 - k, 4)], sem_y.at[k - 1])
    spread("s")
    spread("e")
    for k in (1, 3, 2):
        await_(f"q{k}")
    for yy in range(4):
        wide = qg[yy].astype(jnp.float32) * SCALE2
        first = wide.astype(jnp.bfloat16)
        q2[yy, :, :HD] = first
        q2[yy, :, HD:] = (wide - first.astype(jnp.float32)).astype(jnp.bfloat16)
    forward("s")
    forward("e")
    forward_far("s")
    forward_far("e")
    spread("o")
    all_here("s")
    all_here("e")

    my_order = order[sec]

    def choose(i):
        for j in range(SEC):
            use_fresh = order[j] <= my_order
            block = pl.ds(i * HALF + j * 256, 256)
            here = pl.ds(i * 256, 256)
            chosen = jnp.where(use_fresh, fresh[j, 0, here, :], stale[j, 0, here, :])
            keys2[block, :HD] = chosen
            keys2[block, HD:] = chosen
            vals2[block, :HD] = jnp.where(use_fresh, fresh[j, 1, here, :], stale[j, 1, here, :])

    def tile_of(t):
        return lax.rem(y + 1 + t, 4), t // 4

    def scores(t, keys, slot):
        yy, half = tile_of(t)
        sbuf[slot, :, : keys.size] = lax.dot_general(
            q2[yy, rows(half * TILE, TILE), :], keys2[keys, :], (((1,), (1,)), ((), ())), preferred_element_type=jnp.float32
        )

    def weigh(keys, slot, best):
        weights = jnp.exp2(sbuf[slot, :, : keys.size] - best).astype(jnp.bfloat16)
        return jnp.dot(weights, vals2[keys, :], preferred_element_type=jnp.float32)

    def largest(keys, slot):
        return jnp.max(sbuf[slot, :, : keys.size], axis=1, keepdims=True)

    def begin(t, slot):
        best = largest(FIRST, slot)
        so_far[t] = weigh(FIRST, slot, best)
        best_so_far[t] = jnp.broadcast_to(best, (TILE, HD))

    def finish(t, slot):
        yy, half = tile_of(t)
        before = best_so_far[t]
        best = jnp.maximum(largest(SECOND, slot), before[:, :1])
        both = weigh(SECOND, slot, best)
        factor = jnp.exp2(before - best)
        total = both[:, HD:] + so_far[t, :, HD:] * factor
        value = (both[:, :HD] + so_far[t, :, :HD] * factor) / total
        return yy, half, value, best + jnp.log2(total)

    def end(t, slot):
        yy, half, value, level = finish(t, slot)
        partial[yy, rows(half * TILE, TILE), :] = value.astype(jnp.bfloat16)
        stats[yy, half] = jnp.transpose(level)[:8]
        own[half] = value
        own_l[half] = level

    def give(t):
        yy, half = tile_of(t)
        here = rows(half * TILE, TILE)
        remote(partial.at[yy, here], got.at[y, here], sem_part.at[half, y], at_y(yy))
        remote(stats.at[yy, half], got_stats.at[y, half], sem_stats.at[half, y], at_y(yy))

    def merge(half):
        here = pl.ds(half * TILE, TILE)
        levels, values = [own_l[half]], [own[half]]
        for k in (1, 3, 2):
            yy = lax.rem(y + k, 4)
            arrived(got.at[yy, here], sem_part.at[half, yy])
            arrived(got_stats.at[yy, half], sem_stats.at[half, yy])
            level = got_stats[yy, half]
            levels.append(jnp.transpose(jnp.broadcast_to(level[:1], (HD, TILE))))
            values.append(got[yy, here, :].astype(jnp.float32))
        top = jnp.maximum(jnp.maximum(levels[0], levels[1]), jnp.maximum(levels[2], levels[3]))
        shares = [jnp.exp2(level - top) for level in levels]
        total = shares[0] + shares[1] + shares[2] + shares[3]
        summed = shares[0] * values[0] + shares[1] * values[1] + shares[2] * values[2] + shares[3] * values[3]
        merged[here, :] = (summed / total).astype(jnp.bfloat16)
        for d in range(8):
            zz = half * 8 + d
            src = merged.at[pl.ds(zz * ROWS, ROWS)]

            @pl.when(zz == z)
            def _():
                pltpu.make_async_copy(src, out.at[:, mine], sem_out.at[0]).start()

            @pl.when(zz != z)
            def _():
                remote(src, out.at[:, mine], sem_out.at[0], at_z(zz))

    choose(0)
    scores(0, FIRST, 0)

    def pair_first(u, _):
        t = u * 2
        scores(t + 1, FIRST, 1)
        begin(t, 0)
        scores(t + 2, FIRST, 0)
        begin(t + 1, 1)
        return 0

    lax.fori_loop(0, 2, pair_first, 0)
    forward("o")
    spread_text()
    lax.fori_loop(2, 3, pair_first, 0)
    forward_far("o")
    scores(7, FIRST, 1)
    begin(6, 0)
    begin(7, 1)
    all_here("o")
    for d in range(1, 4):
        await_(f"t{d}")
    choose(1)
    keys2[2 * HALF :, :HD] = text[0]
    keys2[2 * HALF :, HD:] = text[0]
    vals2[2 * HALF :, :HD] = text[1]
    scores(0, SECOND, 0)

    def pair_second(u, _):
        t = u * 2
        scores(t + 1, SECOND, 1)
        end(t, 0)
        scores(t + 2, SECOND, 0)
        end(t + 1, 1)
        give(t)

        @pl.when(u != 1)
        def _():
            give(t + 1)

        return 0

    lax.fori_loop(0, 3, pair_second, 0)
    scores(7, SECOND, 1)
    end(6, 0)
    give(6)
    merge(0)
    end(7, 1)
    merge(1)

    arrived(out, sem_out.at[0])
    count[0] += 6 * 8 + 6 + 15
    assert not pending
    n, rest = divmod(count[0], 16)
    for _ in range(n):
        arrived(qg.at[0], sem_send.at[0])
    if rest:
        arrived(qg.at[0, pl.ds(0, rest * ROWS)], sem_send.at[0])

    @pl.when(high == x)
    def _():
        arrived(qg.at[0, pl.ds(0, 6 * ROWS)], sem_send.at[0])


def local(queries, fresh_keys, fresh_values, stale_keys, stale_values, text_keys, text_values, order):
    anywhere = pl.BlockSpec(memory_space=pl.ANY)
    dma = pltpu.SemaphoreType.DMA
    bf16, f32 = jnp.bfloat16, jnp.float32
    return pl.pallas_call(
        kernel,
        out_shape=jax.ShapeDtypeStruct((ROWS, 16 * HD), bf16),
        in_specs=[anywhere] * 7 + [pl.BlockSpec(memory_space=pltpu.SMEM)],
        out_specs=anywhere,
        scratch_shapes=[
            pltpu.VMEM((4, GROUP, HD), bf16),
            pltpu.VMEM((SEC, 2, GROUP, HD), bf16),
            pltpu.VMEM((SEC, 2, GROUP, HD), bf16),
            pltpu.VMEM((4, 2, 128, HD), bf16),
            pltpu.VMEM((2, TXT, HD), bf16),
            pltpu.VMEM((KEYS, 2 * HD), bf16),
            pltpu.VMEM((KEYS, 2 * HD), bf16),
            pltpu.VMEM((4, GROUP, 2 * HD), bf16),
            pltpu.VMEM((2, TILE, HALF + TXT), f32),
            pltpu.VMEM((8, TILE, 2 * HD), f32),
            pltpu.VMEM((8, TILE, HD), f32),
            pltpu.VMEM((4, GROUP, HD), bf16),
            pltpu.VMEM((4, 2, 8, TILE), f32),
            pltpu.VMEM((4, GROUP, HD), bf16),
            pltpu.VMEM((4, 2, 8, TILE), f32),
            pltpu.VMEM((2, TILE, HD), f32),
            pltpu.VMEM((2, TILE, HD), f32),
            pltpu.VMEM((GROUP, HD), bf16),
            dma((1,)),
            dma((1,)),
            dma((2,)),
            dma((4,)),
            dma((1,)),
            dma((3, 9)),
            dma((3,)),
            dma((3,)),
            dma((2, 4)),
            dma((2, 4)),
            dma((1,)),
        ],
        compiler_params=pltpu.CompilerParams(collective_id=0, has_side_effects=True, vmem_limit_bytes=56 << 20),
    )(queries, fresh_keys, fresh_values, stale_keys, stale_values, text_keys, text_values, order)


def solution(mesh):
    return jax.shard_map(
        local,
        mesh=mesh,
        in_specs=(
            P(("section", "sp", "cfg"), None),
            P(("section", "sp", "cfg"), None),
            P(("section", "sp", "cfg"), None),
            P("sp", ("section", "cfg"), None),
            P("sp", ("section", "cfg"), None),
            P("sp", None),
            P("sp", None),
            P(),
        ),
        out_specs=P(("section", "sp", "cfg"), None),
        check_vma=False,
    )
```
